32 devices in a mesh: seq: 16 (over z, y, core), head: 2 (over x).
Axes of the slice: x: 2, y: 2, z: 4, core: 2. Of those that a mesh axis runs over, the one named last changes fastest.
Arguments:
- queries: bfloat16 [4096, 8192], P(('seq', 'head')), may hold values from -6 to 6
- key_rows: bfloat16 [4096, 1024], P(('seq', 'head')), may hold values from -6 to 6
- value_rows: bfloat16 [4096, 1024], P(('seq', 'head')), may hold values from -6 to 6
- parent: int32 [32], replicated, may hold values from -1 to 30, as said below
Outputs:
- attended: bfloat16 [4096, 8192], P(('seq', 'head'))
The draws below stay inside these ranges and needn't reach their ends.
Inputs may be any that keep to these rules, and one draw needn't show every extreme that they name: parent[b] is -1 exactly for block 0, otherwise an earlier block; the lineage of every block has at most 12 entries, and some block's lineage has exactly 12.
All inputs are finite; a program needn't handle non-finite values.
Results may differ from the reference program's by a relative error of at most 0.005.
Values may be sent and summed in bfloat16 or wider, within the bound.
A program may use at most 64 MiB of HBM per device.

```python
import math
import jax
import jax.numpy as jnp
from jax import lax

HEADS = 64
KV_HEADS = 8
HEAD_DIM = 128
BLOCK = 128
DEPTH = 12
TOKENS = 4096
NBLK = 32
PROB_BLK = 32


def draw_queries(key, part):
    normals = jax.random.normal(jax.random.fold_in(key, 1), (TOKENS, HEADS * HEAD_DIM), jnp.float32)
    return jnp.clip(normals, -6.0, 6.0).astype(jnp.bfloat16)


def draw_key_rows(key, part):
    normals = jax.random.normal(jax.random.fold_in(key, 2), (TOKENS, KV_HEADS * HEAD_DIM), jnp.float32)
    return jnp.clip(normals, -6.0, 6.0).astype(jnp.bfloat16)


def one_problem(problem_key, offset):
    counter = jnp.arange(PROB_BLK, dtype=jnp.int32)

    def place(depths, position):
        roll_key = jax.random.fold_in(problem_key, position)
        proceed = jax.random.randint(jax.random.fold_in(roll_key, 1), (), 0, 4) < 3
        scores = jax.random.randint(jax.random.fold_in(roll_key, 2), (PROB_BLK,), 0, 1 << 20) * PROB_BLK + counter
        allowed = (counter < position) & (depths < DEPTH)
        branch_pick = jnp.argmax(jnp.where(allowed, scores, -1)).astype(jnp.int32)
        previous = jnp.maximum(position - 1, 0)
        prev_depth = lax.dynamic_index_in_dim(depths, previous, 0, keepdims=False)
        keep_on = (position < DEPTH) | proceed & (prev_depth < DEPTH)
        chosen = jnp.where(keep_on, previous, branch_pick)
        chosen = jnp.where(position == 0, -1, chosen).astype(jnp.int32)
        parent_depth = lax.dynamic_index_in_dim(depths, jnp.maximum(chosen, 0), 0, keepdims=False)
        new_depth = jnp.where(position == 0, 1, parent_depth + 1).astype(jnp.int32)
        depths = lax.dynamic_update_index_in_dim(depths, new_depth, position, 0)
        return (depths, chosen)
    unused_depths, parents = lax.scan(place, jnp.zeros((PROB_BLK,), jnp.int32), counter)
    return jnp.where(parents >= 0, parents + offset, -1).astype(jnp.int32)


def draw_parent(key, part):
    problems = NBLK // PROB_BLK
    indices = jnp.arange(problems, dtype=jnp.int32)
    stacked = jax.vmap(lambda which: one_problem(jax.random.fold_in(key, which), which * PROB_BLK))(indices)
    return stacked.reshape(NBLK).astype(jnp.int32)


def shard_levels(stream_key, extent, split, low, top_value):
    factor_of, own = 1.0, jax.random.fold_in(stream_key, 6)
    for axis_at, parts in split:
        heights = jnp.exp(jax.random.uniform(jax.random.fold_in(own, axis_at), (parts,), jnp.float32, low / len(split), top_value / len(split)))
        factor_of = factor_of * jnp.repeat(heights, extent[axis_at] // parts).reshape([-1 if axis == axis_at else 1 for axis in range(len(extent))])
    return factor_of


def scatter_about(key, shape, scale, bound, pieces=(), held_as=jnp.bfloat16):
    entries = jax.random.normal(key, shape, jnp.float32) * scale
    if len(pieces) > 0:
        entries = shard_levels(key, shape, pieces, -0.22, 0.18) * entries
    return jnp.clip(entries, min=-bound, max=bound).astype(held_as)


def setup_inputs(seed: int = 0) -> dict:
    key_of = jax.random.split(jax.random.key(seed), 5)
    return {
        "queries": draw_queries(jax.random.fold_in(key_of[4], 71), 0),
        "key_rows": draw_key_rows(jax.random.fold_in(key_of[4], 71), 0),
        "value_rows": scatter_about(key_of[2], (TOKENS, KV_HEADS * HEAD_DIM), 1.0, 6.0, ((0, 32),)),
        "parent": draw_parent(jax.random.fold_in(key_of[4], 71), 0),
    }


def reference(queries, key_rows, value_rows, parent):
    num_blocks = parent.shape[0]
    per_group = HEADS // KV_HEADS
    inv_root = 1.0 / math.sqrt(HEAD_DIM)
    current = jnp.arange(num_blocks, dtype=jnp.int32)
    lineage = [current]
    for generation in range(DEPTH - 1):
        current = jnp.where(current >= 0, parent[jnp.maximum(current, 0)], -1).astype(jnp.int32)
        lineage.append(current)
    lineage = jnp.stack(lineage, axis=1)
    key_blocks = key_rows.reshape(num_blocks, BLOCK, KV_HEADS, HEAD_DIM)
    value_blocks = value_rows.reshape(num_blocks, BLOCK, KV_HEADS, HEAD_DIM)
    positions = jnp.arange(BLOCK, dtype=jnp.int32)
    causal = positions[None, :] <= positions[:, None]
    levels = jnp.arange(DEPTH, dtype=jnp.int32)

    def one_block(block_id):
        query_rows = lax.dynamic_slice_in_dim(queries, block_id * BLOCK, BLOCK, 0)
        query_rows = query_rows.astype(jnp.float32).reshape(BLOCK, KV_HEADS, per_group, HEAD_DIM)
        ancestors = lax.dynamic_index_in_dim(lineage, block_id, 0, keepdims=False)
        clipped = jnp.maximum(ancestors, 0)
        near_keys = key_blocks[clipped].astype(jnp.float32)
        near_values = value_blocks[clipped].astype(jnp.float32)
        scores = jnp.einsum('qvgd,nkvd->qvgnk', query_rows, near_keys) * inv_root
        visible = (ancestors >= 0)[None, :, None] & ((levels > 0)[None, :, None] | causal[:, None, :])
        scores = jnp.where(visible[:, None, None], scores, -jnp.inf)
        row_max = lax.optimization_barrier(jnp.max(scores, axis=(3, 4), keepdims=True))
        weights = jnp.exp(scores - row_max)
        row_total = lax.optimization_barrier(jnp.sum(weights, axis=(3, 4)))
        rounded = lax.optimization_barrier(weights.astype(jnp.bfloat16)).astype(jnp.float32)
        combined = jnp.einsum('qvgnk,nkvd->qvgd', rounded, near_values)
        return (combined / row_total[..., None]).reshape(BLOCK, HEADS * HEAD_DIM).astype(jnp.bfloat16)
    blocks = lax.map(one_block, jnp.arange(num_blocks, dtype=jnp.int32))
    return blocks.reshape(num_blocks * BLOCK, HEADS * HEAD_DIM)
```

```python
import functools
import math

import jax
import jax.numpy as jnp
from jax import lax
from jax.experimental import pallas as pl
from jax.experimental.pallas import tpu as pltpu
from jax.sharding import PartitionSpec as P

HEADS = 64
KV_HEADS = 8
HEAD_DIM = 128
BLOCK = 128
DEPTH = 12
GROUP = HEADS // KV_HEADS
CHUNKS = 1


def ancestry(parent, first_block, num_local):
    columns = lax.broadcasted_iota(jnp.int32, (num_local, parent.shape[0]), 1)
    current = first_block + jnp.arange(num_local, dtype=jnp.int32)
    lineage = [current]
    for generation in range(DEPTH - 1):
        located = jnp.sum(jnp.where(columns == current[:, None], parent[None, :], 0), axis=1)
        current = jnp.where(current >= 0, located, -1)
        lineage.append(current)
    return jnp.stack(lineage, axis=1)


def attention_kernel(lineage_ref, q_ref, *refs):
    key_refs, value_refs, out_ref = refs[:DEPTH], refs[DEPTH : 2 * DEPTH], refs[2 * DEPTH]
    block = pl.program_id(0)
    keys = jnp.concatenate([ref[...] for ref in key_refs], axis=0)
    values = jnp.concatenate([ref[...] for ref in value_refs], axis=0)
    factor = math.log2(math.e) / math.sqrt(HEAD_DIM)
    per_dot = 2
    rows = per_dot * BLOCK
    row = lax.rem(lax.broadcasted_iota(jnp.int32, (rows, BLOCK), 0), BLOCK)
    causal = lax.broadcasted_iota(jnp.int32, (rows, BLOCK), 1) <= row
    penalties = [
        jnp.where(lineage_ref[block, level] >= 0, 0.0, -jnp.inf).astype(jnp.float32)
        for level in range(DEPTH)
    ]
    for part in range(GROUP // per_dot):
        heads = range(part * per_dot, (part + 1) * per_dot)
        query = jnp.concatenate(
            [q_ref[:, head * HEAD_DIM : (head + 1) * HEAD_DIM] for head in heads], axis=0
        )
        scores = lax.dot_general(
            query, keys, (((1,), (1,)), ((), ())), preferred_element_type=jnp.float32
        )
        tiles = []
        for level in range(DEPTH):
            tile = scores[:, level * BLOCK : (level + 1) * BLOCK]
            if level == 0:
                tile = jnp.where(causal, tile, -jnp.inf)
            else:
                tile = tile + penalties[level]
            tiles.append(tile)
        peak = functools.reduce(jnp.maximum, tiles)
        peak = jnp.max(peak, axis=1, keepdims=True)
        weights = [jnp.exp2((tile - peak) * factor) for tile in tiles]
        total = jnp.sum(functools.reduce(jnp.add, weights), axis=1, keepdims=True)
        rounded = jnp.concatenate([weight.astype(jnp.bfloat16) for weight in weights], axis=1)
        result = jnp.dot(rounded, values, preferred_element_type=jnp.float32) / total
        for at, head in enumerate(heads):
            out_ref[:, head * HEAD_DIM : (head + 1) * HEAD_DIM] = result[
                at * BLOCK : (at + 1) * BLOCK
            ].astype(out_ref.dtype)


def attention(lineage, queries, keys, values, key_at, value_at, kv_heads):
    num_local = queries.shape[0] // BLOCK

    def tile_spec(level, first):
        return pl.BlockSpec(
            (BLOCK, HEAD_DIM),
            lambda block, head, lineage: (jnp.maximum(lineage[block, level], 0), first + head),
        )

    wide = pl.BlockSpec((BLOCK, GROUP * HEAD_DIM), lambda block, head, lineage: (block, head))
    return pl.pallas_call(
        attention_kernel,
        grid_spec=pltpu.PrefetchScalarGridSpec(
            num_scalar_prefetch=1,
            grid=(num_local, kv_heads),
            in_specs=[wide]
            + [tile_spec(level, key_at) for level in range(DEPTH)]
            + [tile_spec(level, value_at) for level in range(DEPTH)],
            out_specs=wide,
        ),
        out_shape=jax.ShapeDtypeStruct(queries.shape, jnp.bfloat16),
        compiler_params=pltpu.CompilerParams(vmem_limit_bytes=48 * 1024 * 1024),
        cost_estimate=pl.CostEstimate(
            flops=4 * queries.size * DEPTH * BLOCK,
            bytes_accessed=4 * queries.size + 4 * num_local * DEPTH * BLOCK * kv_heads * HEAD_DIM,
            transcendentals=queries.size * DEPTH,
        ),
    )(lineage, queries, *([keys] * DEPTH), *([values] * DEPTH))


def local_body(queries, key_rows, value_rows, parent):
    device = lax.axis_index("seq") * lax.axis_size("head") + lax.axis_index("head")
    num_local = queries.shape[0] // BLOCK
    lineage = ancestry(parent, device * num_local, num_local)
    both = jnp.concatenate([key_rows, value_rows], axis=1)
    gathered = lax.all_gather(both, ("seq", "head"), axis=0, tiled=True)
    return attention(lineage, queries, gathered, gathered, 0, KV_HEADS, KV_HEADS)


def split_body(queries, key_rows, value_rows, parent):
    exchange = functools.partial(
        lax.all_to_all, axis_name="head", split_axis=1, concat_axis=0, tiled=True
    )
    kv_heads = KV_HEADS // lax.axis_size("head")
    q_local, k_local, v_local = exchange(queries), exchange(key_rows), exchange(value_rows)
    num_local = q_local.shape[0] // BLOCK
    lineage = ancestry(parent, lax.axis_index("seq") * num_local, num_local)
    keys = lax.all_gather(k_local, "seq", axis=0, tiled=True)
    values = lax.all_gather(v_local, "seq", axis=0, tiled=True)
    attended = attention(lineage, q_local, keys, values, 0, 0, kv_heads)
    return lax.all_to_all(attended, "head", split_axis=0, concat_axis=1, tiled=True)


def body(queries, key_rows, value_rows, parent):
    if queries.shape[0] % BLOCK == 0:
        return local_body(queries, key_rows, value_rows, parent)
    return split_body(queries, key_rows, value_rows, parent)


def solution(mesh):
    return jax.shard_map(
        body,
        mesh=mesh,
        in_specs=(
            P(("seq", "head"), None),
            P(("seq", "head"), None),
            P(("seq", "head"), None),
            P(),
        ),
        out_specs=P(("seq", "head"), None),
        check_vma=False,
    )
```

```python
import functools
import math

import jax
import jax.numpy as jnp
from jax import lax
from jax.experimental import pallas as pl
from jax.experimental.pallas import tpu as pltpu
from jax.sharding import PartitionSpec as P

HEADS = 64
KV_HEADS = 8
HEAD_DIM = 128
BLOCK = 128
DEPTH = 12
GROUP = HEADS // KV_HEADS
CHUNKS = 4
PER_DOT = 2
PORTIONS = 2
MESH = pl.DeviceIdType.MESH


def ancestry(parent, first_block, num_local):
    columns = lax.broadcasted_iota(jnp.int32, (num_local, parent.shape[0]), 1)
    current = first_block + jnp.arange(num_local, dtype=jnp.int32)
    lineage = [current]
    for generation in range(DEPTH - 1):
        located = jnp.sum(jnp.where(columns == current[:, None], parent[None, :], 0), axis=1)
        current = jnp.where(current >= 0, located, -1)
        lineage.append(current)
    return jnp.stack(lineage, axis=1)


def attention_kernel(lineage_ref, q_ref, *refs):
    key_refs, value_refs, out_ref = refs[:DEPTH], refs[DEPTH : 2 * DEPTH], refs[2 * DEPTH]
    block = pl.program_id(0)
    keys = jnp.concatenate([ref[...] for ref in key_refs], axis=0)
    values = jnp.concatenate([ref[...] for ref in value_refs], axis=0)
    factor = math.log2(math.e) / math.sqrt(HEAD_DIM)
    per_dot = 2
    rows = per_dot * BLOCK
    row = lax.rem(lax.broadcasted_iota(jnp.int32, (rows, BLOCK), 0), BLOCK)
    causal = lax.broadcasted_iota(jnp.int32, (rows, BLOCK), 1) <= row
    penalties = [
        jnp.where(lineage_ref[block, level] >= 0, 0.0, -jnp.inf).astype(jnp.float32)
        for level in range(DEPTH)
    ]
    for part in range(GROUP // per_dot):
        heads = range(part * per_dot, (part + 1) * per_dot)
        query = jnp.concatenate(
            [q_ref[:, head * HEAD_DIM : (head + 1) * HEAD_DIM] for head in heads], axis=0
        )
        scores = lax.dot_general(
            query, keys, (((1,), (1,)), ((), ())), preferred_element_type=jnp.float32
        )
        tiles = []
        for level in range(DEPTH):
            tile = scores[:, level * BLOCK : (level + 1) * BLOCK]
            if level == 0:
                tile = jnp.where(causal, tile, -jnp.inf)
            else:
                tile = tile + penalties[level]
            tiles.append(tile)
        peak = functools.reduce(jnp.maximum, tiles)
        peak = jnp.max(peak, axis=1, keepdims=True)
        weights = [jnp.exp2((tile - peak) * factor) for tile in tiles]
        total = jnp.sum(functools.reduce(jnp.add, weights), axis=1, keepdims=True)
        rounded = jnp.concatenate([weight.astype(jnp.bfloat16) for weight in weights], axis=1)
        result = jnp.dot(rounded, values, preferred_element_type=jnp.float32) / total
        for at, head in enumerate(heads):
            out_ref[:, head * HEAD_DIM : (head + 1) * HEAD_DIM] = result[
                at * BLOCK : (at + 1) * BLOCK
            ].astype(out_ref.dtype)


def attention(lineage, queries, keys, values, key_at, value_at, kv_heads):
    num_local = queries.shape[0] // BLOCK

    def tile_spec(level, first):
        return pl.BlockSpec(
            (BLOCK, HEAD_DIM),
            lambda block, head, lineage: (jnp.maximum(lineage[block, level], 0), first + head),
        )

    wide = pl.BlockSpec((BLOCK, GROUP * HEAD_DIM), lambda block, head, lineage: (block, head))
    return pl.pallas_call(
        attention_kernel,
        grid_spec=pltpu.PrefetchScalarGridSpec(
            num_scalar_prefetch=1,
            grid=(num_local, kv_heads),
            in_specs=[wide]
            + [tile_spec(level, key_at) for level in range(DEPTH)]
            + [tile_spec(level, value_at) for level in range(DEPTH)],
            out_specs=wide,
        ),
        out_shape=jax.ShapeDtypeStruct(queries.shape, jnp.bfloat16),
        compiler_params=pltpu.CompilerParams(vmem_limit_bytes=48 * 1024 * 1024),
        cost_estimate=pl.CostEstimate(
            flops=4 * queries.size * DEPTH * BLOCK,
            bytes_accessed=4 * queries.size + 4 * num_local * DEPTH * BLOCK * kv_heads * HEAD_DIM,
            transcendentals=queries.size * DEPTH,
        ),
    )(lineage, queries, *([keys] * DEPTH), *([values] * DEPTH))


def fused_kernel(planes, parent_ref, q_ref, k_ref, v_ref, out_ref, *scratch):
    buffers, (send_sems, recv_sems) = scratch[:CHUNKS], scratch[CHUNKS:]
    seq, x = lax.axis_index("seq"), lax.axis_index("head")
    z, y, core = seq // 4, lax.rem(seq // 2, 2), lax.rem(seq, 2)
    block = seq * 2 + x
    rows = q_ref.shape[0]
    width = KV_HEADS * HEAD_DIM // (2 * CHUNKS)

    def place(zz, yy, cc, xx):
        return (zz * 4 + yy * 2 + cc, xx)

    above, below = place(z + 1, y, core, x), place(z - 1, y, core, x)
    across_x, across_y = place(z, y, core, 1 - x), place(z, 1 - y, core, x)
    sibling = place(z, y, 1 - core, x)

    barrier = pltpu.get_barrier_semaphore()

    def greet(target):
        pl.semaphore_signal(barrier, inc=1, device_id=target, device_id_type=MESH)

    for target in (across_x, across_y, sibling):
        greet(target)

    @pl.when(z > 0)
    def _():
        greet(below)

    @pl.when(z < planes - 1)
    def _():
        greet(above)

    for chunk in range(CHUNKS):
        for part in range(4):
            source = (k_ref, v_ref)[part % 2]
            first, second = ((x, y), (y, x))[part % 2]
            at = (chunk * 2 + part // 2) * width
            slot = z * 8 + core * 4 + second * 2 + first
            buffers[chunk][part, slot] = source[:, at : at + width]

    lineage = [block]
    for level in range(DEPTH - 1):
        found = parent_ref[jnp.maximum(lineage[-1], 0)]
        lineage.append(jnp.where(lineage[-1] >= 0, found, -1))
    penalties = [jnp.where(b >= 0, 0.0, -jnp.inf).astype(jnp.float32) for b in lineage]
    clipped = [jnp.maximum(b, 0) for b in lineage]
    key_slots, value_slots = [], []
    for b in clipped:
        bz, by, bc, bx = b // 8, lax.rem(b // 4, 2), lax.rem(b // 2, 2), lax.rem(b, 2)
        key_slots.append(bz * 8 + bc * 4 + by * 2 + bx)
        value_slots.append(bz * 8 + bc * 4 + bx * 2 + by)

    pl.semaphore_wait(barrier, 3 + (z > 0).astype(jnp.int32) + (z < planes - 1).astype(jnp.int32))

    def copy(chunk, part, zz, stage, slot, count, target):
        span = buffers[chunk].at[part, pl.ds(slot, count)]
        return pltpu.make_async_remote_copy(
            src_ref=span,
            dst_ref=span,
            send_sem=send_sems.at[chunk, part, zz, stage],
            recv_sem=recv_sems.at[chunk, part, zz, stage],
            device_id=target,
            device_id_type=MESH,
        )

    def routes(part):
        if part % 2 == 0:
            return x, y, across_x, across_y
        return y, x, across_y, across_x

    def hop_up(chunk, part, zz):
        first, second, _, _ = routes(part)
        base = zz * 8 + core * 4 + second * 2
        if part < 2:
            return copy(chunk, part, zz, 0, base + first, 1, above)
        return copy(chunk, part, zz, 0, base, 2, above)

    def hop_first(chunk, part, zz, mine):
        first, second, target, _ = routes(part)
        at = first if mine else 1 - first
        return copy(chunk, part, zz, 1, zz * 8 + core * 4 + second * 2 + at, 1, target)

    def hop_second(chunk, part, zz, mine):
        _, second, _, target = routes(part)
        at = second if mine else 1 - second
        return copy(chunk, part, zz, 2, zz * 8 + core * 4 + at * 2, 2, target)

    def hop_core(chunk, part, zz, mine):
        at = core if mine else 1 - core
        return copy(chunk, part, zz, 3, zz * 8 + at * 4, 4, sibling)

    def rise(chunk, part, zz):
        @pl.when(z < planes - 1)
        def _():
            hop_up(chunk, part, zz).start()

    def step_a(chunk, age):
        zz = z - age
        for part in (2, 3, 0, 1):
            if age > 0:
                hop_up(chunk, part, zz).wait_recv()
            if part < 2:
                rise(chunk, part, zz)
                hop_first(chunk, part, zz, True).start()
            elif age == 0:
                hop_first(chunk, part, zz, True).start()
            else:
                rise(chunk, part, zz)
                hop_second(chunk, part, zz, True).start()

    def step_b(chunk, age):
        zz = z - age
        for part in (2, 3, 0, 1):
            if part < 2 or age == 0:
                hop_first(chunk, part, zz, False).wait_recv()
                if part >= 2:
                    rise(chunk, part, zz)
                hop_second(chunk, part, zz, True).start()

    def step_c(chunk, age):
        for part in (2, 3, 0, 1):
            hop_second(chunk, part, z - age, False).wait_recv()
            hop_core(chunk, part, z - age, True).start()

    def step_d(chunk, age):
        for part in (2, 3, 0, 1):
            hop_core(chunk, part, z - age, False).wait_recv()

    def guarded(step, chunk, age):
        if age == 0:
            step(chunk, age)
        else:
            pl.when(z >= age)(functools.partial(step, chunk, age))

    factor = math.log2(math.e) / math.sqrt(HEAD_DIM)
    wide_rows = PER_DOT * rows
    row = lax.rem(lax.broadcasted_iota(jnp.int32, (wide_rows, BLOCK), 0), BLOCK)
    causal = lax.broadcasted_iota(jnp.int32, (wide_rows, BLOCK), 1) <= row

    def attend(chunk, kv_head, portion):
        pair, lane = divmod(kv_head, width // HEAD_DIM)
        lanes = pl.ds(lane * HEAD_DIM, HEAD_DIM)
        buffer = buffers[chunk]
        keys = jnp.concatenate([buffer[2 * pair, slot, :, lanes] for slot in key_slots], axis=0)
        values = jnp.concatenate(
            [buffer[2 * pair + 1, slot, :, lanes] for slot in value_slots], axis=0
        )
        first_head = (chunk * (KV_HEADS // CHUNKS) + kv_head) * GROUP
        dots = GROUP // PER_DOT // PORTIONS
        for dot_at in range(portion * dots, (portion + 1) * dots):
            heads = [first_head + dot_at * PER_DOT + i for i in range(PER_DOT)]
            query = jnp.concatenate(
                [q_ref[:, head * HEAD_DIM : (head + 1) * HEAD_DIM] for head in heads], axis=0
            )
            scores = lax.dot_general(
                query, keys, (((1,), (1,)), ((), ())), preferred_element_type=jnp.float32
            )
            tiles = []
            for level in range(DEPTH):
                tile = scores[:, level * BLOCK : (level + 1) * BLOCK]
                if level == 0:
                    tile = jnp.where(causal, tile, -jnp.inf)
                else:
                    tile = tile + penalties[level]
                tiles.append(tile)
            peak = jnp.max(functools.reduce(jnp.maximum, tiles), axis=1, keepdims=True)
            weights = [jnp.exp2((tile - peak) * factor) for tile in tiles]
            total = jnp.sum(functools.reduce(jnp.add, weights), axis=1, keepdims=True)
            rounded = jnp.concatenate([w.astype(jnp.bfloat16) for w in weights], axis=1)
            result = jnp.dot(rounded, values, preferred_element_type=jnp.float32) / total
            for i, head in enumerate(heads):
                out_ref[:, head * HEAD_DIM : (head + 1) * HEAD_DIM] = result[
                    i * rows : (i + 1) * rows
                ].astype(out_ref.dtype)

    items = [(chunk, age) for chunk in range(CHUNKS) for age in range(planes)]
    pending = []
    for at in range(len(items) + 3):
        for delay, step in ((3, step_d), (2, step_c), (1, step_b), (0, step_a)):
            if 0 <= at - delay < len(items):
                guarded(step, *items[at - delay])
        if at >= 3 and items[at - 3][1] == planes - 1:
            chunk = items[at - 3][0]
            for kv_head in range(KV_HEADS // CHUNKS):
                for portion in range(PORTIONS):
                    pending.append((chunk, kv_head, portion))
        for _ in range(-(-KV_HEADS * PORTIONS // len(items))):
            if pending:
                attend(*pending.pop(0))
    for work in pending:
        attend(*work)

    for chunk in range(CHUNKS):
        for age in range(planes):

            def finish(chunk, age):
                zz = z - age
                for part in range(4):
                    if part < 2 or age == 0:
                        hop_first(chunk, part, zz, True).wait_send()
                    hop_second(chunk, part, zz, True).wait_send()
                    hop_core(chunk, part, zz, True).wait_send()

                    @pl.when(z < planes - 1)
                    def _():
                        hop_up(chunk, part, zz).wait_send()

            guarded(finish, chunk, age)


def fused_body(queries, key_rows, value_rows, parent):
    devices = lax.axis_size("seq") * lax.axis_size("head")
    planes = devices // 8
    width = KV_HEADS * HEAD_DIM // (2 * CHUNKS)
    vmem = pl.BlockSpec(memory_space=pltpu.VMEM)
    return pl.pallas_call(
        functools.partial(fused_kernel, planes),
        out_shape=jax.ShapeDtypeStruct(queries.shape, jnp.bfloat16),
        in_specs=[pl.BlockSpec(memory_space=pltpu.SMEM), vmem, vmem, vmem],
        out_specs=vmem,
        scratch_shapes=[pltpu.VMEM((4, devices, BLOCK, width), jnp.bfloat16)] * CHUNKS
        + [pltpu.SemaphoreType.DMA((CHUNKS, 4, planes, 4))] * 2,
        compiler_params=pltpu.CompilerParams(
            collective_id=0, has_side_effects=True, vmem_limit_bytes=56 * 1024 * 1024
        ),
        cost_estimate=pl.CostEstimate(
            flops=4 * queries.size * DEPTH * BLOCK,
            bytes_accessed=4 * queries.size,
            transcendentals=queries.size * DEPTH,
        ),
    )(parent, queries, key_rows, value_rows)


def split_body(queries, key_rows, value_rows, parent):
    exchange = functools.partial(
        lax.all_to_all, axis_name="head", split_axis=1, concat_axis=0, tiled=True
    )
    kv_heads = KV_HEADS // lax.axis_size("head")
    q_local, k_local, v_local = exchange(queries), exchange(key_rows), exchange(value_rows)
    num_local = q_local.shape[0] // BLOCK
    lineage = ancestry(parent, lax.axis_index("seq") * num_local, num_local)
    keys = lax.all_gather(k_local, "seq", axis=0, tiled=True)
    values = lax.all_gather(v_local, "seq", axis=0, tiled=True)
    attended = attention(lineage, q_local, keys, values, 0, 0, kv_heads)
    return lax.all_to_all(attended, "head", split_axis=0, concat_axis=1, tiled=True)


def body(queries, key_rows, value_rows, parent):
    seq, head = lax.axis_size("seq"), lax.axis_size("head")
    if queries.shape[0] == BLOCK and head == 2 and seq % 4 == 0 and seq <= 16:
        return fused_body(queries, key_rows, value_rows, parent)
    return split_body(queries, key_rows, value_rows, parent)


def solution(mesh):
    return jax.shard_map(
        body,
        mesh=mesh,
        in_specs=(
            P(("seq", "head"), None),
            P(("seq", "head"), None),
            P(("seq", "head"), None),
            P(),
        ),
        out_specs=P(("seq", "head"), None),
        check_vma=False,
    )
```

```python
import functools
import math

import jax
import jax.numpy as jnp
from jax import lax
from jax.experimental import pallas as pl
from jax.experimental.pallas import tpu as pltpu
from jax.sharding import PartitionSpec as P

HEADS = 64
KV_HEADS = 8
HEAD_DIM = 128
BLOCK = 128
DEPTH = 12
GROUP = HEADS // KV_HEADS
CHUNKS = 4
PER_DOT = 2
PORTIONS = 2
DIRECT = 4
MESH = pl.DeviceIdType.MESH


def ancestry(parent, first_block, num_local):
    columns = lax.broadcasted_iota(jnp.int32, (num_local, parent.shape[0]), 1)
    current = first_block + jnp.arange(num_local, dtype=jnp.int32)
    lineage = [current]
    for generation in range(DEPTH - 1):
        located = jnp.sum(jnp.where(columns == current[:, None], parent[None, :], 0), axis=1)
        current = jnp.where(current >= 0, located, -1)
        lineage.append(current)
    return jnp.stack(lineage, axis=1)


def attention_kernel(lineage_ref, q_ref, *refs):
    key_refs, value_refs, out_ref = refs[:DEPTH], refs[DEPTH : 2 * DEPTH], refs[2 * DEPTH]
    block = pl.program_id(0)
    keys = jnp.concatenate([ref[...] for ref in key_refs], axis=0)
    values = jnp.concatenate([ref[...] for ref in value_refs], axis=0)
    factor = math.log2(math.e) / math.sqrt(HEAD_DIM)
    per_dot = 2
    rows = per_dot * BLOCK
    row = lax.rem(lax.broadcasted_iota(jnp.int32, (rows, BLOCK), 0), BLOCK)
    causal = lax.broadcasted_iota(jnp.int32, (rows, BLOCK), 1) <= row
    penalties = [
        jnp.where(lineage_ref[block, level] >= 0, 0.0, -jnp.inf).astype(jnp.float32)
        for level in range(DEPTH)
    ]
    for part in range(GROUP // per_dot):
        heads = range(part * per_dot, (part + 1) * per_dot)
        query = jnp.concatenate(
            [q_ref[:, head * HEAD_DIM : (head + 1) * HEAD_DIM] for head in heads], axis=0
        )
        scores = lax.dot_general(
            query, keys, (((1,), (1,)), ((), ())), preferred_element_type=jnp.float32
        )
        tiles = []
        for level in range(DEPTH):
            tile = scores[:, level * BLOCK : (level + 1) * BLOCK]
            if level == 0:
                tile = jnp.where(causal, tile, -jnp.inf)
            else:
                tile = tile + penalties[level]
            tiles.append(tile)
        peak = functools.reduce(jnp.maximum, tiles)
        peak = jnp.max(peak, axis=1, keepdims=True)
        weights = [jnp.exp2((tile - peak) * factor) for tile in tiles]
        total = jnp.sum(functools.reduce(jnp.add, weights), axis=1, keepdims=True)
        rounded = jnp.concatenate([weight.astype(jnp.bfloat16) for weight in weights], axis=1)
        result = jnp.dot(rounded, values, preferred_element_type=jnp.float32) / total
        for at, head in enumerate(heads):
            out_ref[:, head * HEAD_DIM : (head + 1) * HEAD_DIM] = result[
                at * BLOCK : (at + 1) * BLOCK
            ].astype(out_ref.dtype)


def attention(lineage, queries, keys, values, key_at, value_at, kv_heads):
    num_local = queries.shape[0] // BLOCK

    def tile_spec(level, first):
        return pl.BlockSpec(
            (BLOCK, HEAD_DIM),
            lambda block, head, lineage: (jnp.maximum(lineage[block, level], 0), first + head),
        )

    wide = pl.BlockSpec((BLOCK, GROUP * HEAD_DIM), lambda block, head, lineage: (block, head))
    return pl.pallas_call(
        attention_kernel,
        grid_spec=pltpu.PrefetchScalarGridSpec(
            num_scalar_prefetch=1,
            grid=(num_local, kv_heads),
            in_specs=[wide]
            + [tile_spec(level, key_at) for level in range(DEPTH)]
            + [tile_spec(level, value_at) for level in range(DEPTH)],
            out_specs=wide,
        ),
        out_shape=jax.ShapeDtypeStruct(queries.shape, jnp.bfloat16),
        compiler_params=pltpu.CompilerParams(vmem_limit_bytes=48 * 1024 * 1024),
        cost_estimate=pl.CostEstimate(
            flops=4 * queries.size * DEPTH * BLOCK,
            bytes_accessed=4 * queries.size + 4 * num_local * DEPTH * BLOCK * kv_heads * HEAD_DIM,
            transcendentals=queries.size * DEPTH,
        ),
    )(lineage, queries, *([keys] * DEPTH), *([values] * DEPTH))


def fused_kernel(planes, parent_ref, q_ref, k_ref, v_ref, out_ref, *scratch):
    buffers, (send_sems, recv_sems) = scratch[:CHUNKS], scratch[CHUNKS:]
    seq, x = lax.axis_index("seq"), lax.axis_index("head")
    z, y, core = seq // 4, lax.rem(seq // 2, 2), lax.rem(seq, 2)
    block = seq * 2 + x
    rows = q_ref.shape[0]
    width = KV_HEADS * HEAD_DIM // (2 * CHUNKS)

    def place(zz, yy, cc, xx):
        return (zz * 4 + yy * 2 + cc, xx)

    above, below = place(z + 1, y, core, x), place(z - 1, y, core, x)
    across_x, across_y = place(z, y, core, 1 - x), place(z, 1 - y, core, x)
    sibling = place(z, y, 1 - core, x)

    barrier = pltpu.get_barrier_semaphore()

    def greet(target):
        pl.semaphore_signal(barrier, inc=1, device_id=target, device_id_type=MESH)

    for target in (across_x, across_y, sibling):
        greet(target)

    @pl.when(z > 0)
    def _():
        greet(below)

    @pl.when(z < planes - 1)
    def _():
        greet(above)

    for chunk in range(CHUNKS):
        for part in range(4):
            source = (k_ref, v_ref)[part % 2]
            first, second = ((x, y), (y, x))[part % 2]
            at = (chunk * 2 + part // 2) * width
            slot = z * 8 + core * 4 + second * 2 + first
            buffers[chunk][part, slot] = source[:, at : at + width]

    lineage = [block]
    for level in range(DEPTH - 1):
        found = parent_ref[jnp.maximum(lineage[-1], 0)]
        lineage.append(jnp.where(lineage[-1] >= 0, found, -1))
    penalties = [jnp.where(b >= 0, 0.0, -jnp.inf).astype(jnp.float32) for b in lineage]
    clipped = [jnp.maximum(b, 0) for b in lineage]
    key_slots, value_slots = [], []
    for b in clipped:
        bz, by, bc, bx = b // 8, lax.rem(b // 4, 2), lax.rem(b // 2, 2), lax.rem(b, 2)
        key_slots.append(bz * 8 + bc * 4 + by * 2 + bx)
        value_slots.append(bz * 8 + bc * 4 + bx * 2 + by)

    pl.semaphore_wait(barrier, 3 + (z > 0).astype(jnp.int32) + (z < planes - 1).astype(jnp.int32))

    def copy(chunk, part, zz, stage, slot, count, target):
        span = buffers[chunk].at[part, pl.ds(slot, count)]
        return pltpu.make_async_remote_copy(
            src_ref=span,
            dst_ref=span,
            send_sem=send_sems.at[chunk, part, zz, stage],
            recv_sem=recv_sems.at[chunk, part, zz, stage],
            device_id=target,
            device_id_type=MESH,
        )

    def routes(part):
        if part % 2 == 0:
            return x, y, across_x, across_y
        return y, x, across_y, across_x

    def hop_up(chunk, part, zz):
        first, second, _, _ = routes(part)
        base = zz * 8 + core * 4 + second * 2
        if part < DIRECT:
            return copy(chunk, part, zz, 0, base + first, 1, above)
        return copy(chunk, part, zz, 0, base, 2, above)

    def hop_first(chunk, part, zz, mine):
        first, second, target, _ = routes(part)
        at = first if mine else 1 - first
        return copy(chunk, part, zz, 1, zz * 8 + core * 4 + second * 2 + at, 1, target)

    def hop_second(chunk, part, zz, mine):
        _, second, _, target = routes(part)
        at = second if mine else 1 - second
        return copy(chunk, part, zz, 2, zz * 8 + core * 4 + at * 2, 2, target)

    def hop_core(chunk, part, zz, mine):
        at = core if mine else 1 - core
        return copy(chunk, part, zz, 3, zz * 8 + at * 4, 4, sibling)

    def rise(chunk, part, zz):
        @pl.when(z < planes - 1)
        def _():
            hop_up(chunk, part, zz).start()

    def step_a(chunk, age):
        zz = z - age
        for part in (2, 3, 0, 1):
            if age > 0:
                hop_up(chunk, part, zz).wait_recv()
            if part < DIRECT:
                rise(chunk, part, zz)
                hop_first(chunk, part, zz, True).start()
            elif age == 0:
                hop_first(chunk, part, zz, True).start()
            else:
                rise(chunk, part, zz)
                hop_second(chunk, part, zz, True).start()

    def step_b(chunk, age):
        zz = z - age
        for part in (2, 3, 0, 1):
            if part < DIRECT or age == 0:
                hop_first(chunk, part, zz, False).wait_recv()
                if part >= DIRECT:
                    rise(chunk, part, zz)
                hop_second(chunk, part, zz, True).start()

    def step_c(chunk, age):
        for part in (2, 3, 0, 1):
            hop_second(chunk, part, z - age, False).wait_recv()
            hop_core(chunk, part, z - age, True).start()

    def step_d(chunk, age):
        for part in (2, 3, 0, 1):
            hop_core(chunk, part, z - age, False).wait_recv()

    def guarded(step, chunk, age):
        if age == 0:
            step(chunk, age)
        else:
            pl.when(z >= age)(functools.partial(step, chunk, age))

    factor = math.log2(math.e) / math.sqrt(HEAD_DIM)
    wide_rows = PER_DOT * rows
    row = lax.rem(lax.broadcasted_iota(jnp.int32, (wide_rows, BLOCK), 0), BLOCK)
    causal = lax.broadcasted_iota(jnp.int32, (wide_rows, BLOCK), 1) <= row

    def attend(chunk, kv_head, portion):
        pair, lane = divmod(kv_head, width // HEAD_DIM)
        lanes = pl.ds(lane * HEAD_DIM, HEAD_DIM)
        buffer = buffers[chunk]
        keys = jnp.concatenate([buffer[2 * pair, slot, :, lanes] for slot in key_slots], axis=0)
        values = jnp.concatenate(
            [buffer[2 * pair + 1, slot, :, lanes] for slot in value_slots], axis=0
        )
        first_head = (chunk * (KV_HEADS // CHUNKS) + kv_head) * GROUP
        dots = GROUP // PER_DOT // PORTIONS
        for dot_at in range(portion * dots, (portion + 1) * dots):
            heads = [first_head + dot_at * PER_DOT + i for i in range(PER_DOT)]
            query = jnp.concatenate(
                [q_ref[:, head * HEAD_DIM : (head + 1) * HEAD_DIM] for head in heads], axis=0
            )
            scores = lax.dot_general(
                query, keys, (((1,), (1,)), ((), ())), preferred_element_type=jnp.float32
            )
            tiles = []
            for level in range(DEPTH):
                tile = scores[:, level * BLOCK : (level + 1) * BLOCK]
                if level == 0:
                    tile = jnp.where(causal, tile, -jnp.inf)
                else:
                    tile = tile + penalties[level]
                tiles.append(tile)
            peak = jnp.max(functools.reduce(jnp.maximum, tiles), axis=1, keepdims=True)
            weights = [jnp.exp2((tile - peak) * factor) for tile in tiles]
            total = jnp.sum(functools.reduce(jnp.add, weights), axis=1, keepdims=True)
            rounded = jnp.concatenate([w.astype(jnp.bfloat16) for w in weights], axis=1)
            result = jnp.dot(rounded, values, preferred_element_type=jnp.float32) / total
            for i, head in enumerate(heads):
                out_ref[:, head * HEAD_DIM : (head + 1) * HEAD_DIM] = result[
                    i * rows : (i + 1) * rows
                ].astype(out_ref.dtype)

    items = [(chunk, age) for chunk in range(CHUNKS) for age in range(planes)]
    items.sort(key=lambda item: item[0] * 4 + item[1] * 2)
    pending = []
    for at in range(len(items) + 6):
        for delay, step in ((6, step_d), (4, step_c), (2, step_b), (0, step_a)):
            if 0 <= at - delay < len(items):
                guarded(step, *items[at - delay])
        if at >= 6 and items[at - 6][1] == planes - 1:
            chunk = items[at - 6][0]
            for kv_head in range(KV_HEADS // CHUNKS):
                for portion in range(PORTIONS):
                    pending.append((chunk, kv_head, portion))
        for _ in range(-(-KV_HEADS * PORTIONS // len(items))):
            if pending:
                attend(*pending.pop(0))
    for work in pending:
        attend(*work)

    for chunk in range(CHUNKS):
        for age in range(planes):

            def finish(chunk, age):
                zz = z - age
                for part in range(4):
                    if part < DIRECT or age == 0:
                        hop_first(chunk, part, zz, True).wait_send()
                    hop_second(chunk, part, zz, True).wait_send()
                    hop_core(chunk, part, zz, True).wait_send()

                    @pl.when(z < planes - 1)
                    def _():
                        hop_up(chunk, part, zz).wait_send()

            guarded(finish, chunk, age)


def fused_body(queries, key_rows, value_rows, parent):
    devices = lax.axis_size("seq") * lax.axis_size("head")
    planes = devices // 8
    width = KV_HEADS * HEAD_DIM // (2 * CHUNKS)
    vmem = pl.BlockSpec(memory_space=pltpu.VMEM)
    return pl.pallas_call(
        functools.partial(fused_kernel, planes),
        out_shape=jax.ShapeDtypeStruct(queries.shape, jnp.bfloat16),
        in_specs=[pl.BlockSpec(memory_space=pltpu.SMEM), vmem, vmem, vmem],
        out_specs=vmem,
        scratch_shapes=[pltpu.VMEM((4, devices, BLOCK, width), jnp.bfloat16)] * CHUNKS
        + [pltpu.SemaphoreType.DMA((CHUNKS, 4, planes, 4))] * 2,
        compiler_params=pltpu.CompilerParams(
            collective_id=0, has_side_effects=True, vmem_limit_bytes=56 * 1024 * 1024
        ),
        cost_estimate=pl.CostEstimate(
            flops=4 * queries.size * DEPTH * BLOCK,
            bytes_accessed=4 * queries.size,
            transcendentals=queries.size * DEPTH,
        ),
    )(parent, queries, key_rows, value_rows)


def split_body(queries, key_rows, value_rows, parent):
    exchange = functools.partial(
        lax.all_to_all, axis_name="head", split_axis=1, concat_axis=0, tiled=True
    )
    kv_heads = KV_HEADS // lax.axis_size("head")
    q_local, k_local, v_local = exchange(queries), exchange(key_rows), exchange(value_rows)
    num_local = q_local.shape[0] // BLOCK
    lineage = ancestry(parent, lax.axis_index("seq") * num_local, num_local)
    keys = lax.all_gather(k_local, "seq", axis=0, tiled=True)
    values = lax.all_gather(v_local, "seq", axis=0, tiled=True)
    attended = attention(lineage, q_local, keys, values, 0, 0, kv_heads)
    return lax.all_to_all(attended, "head", split_axis=0, concat_axis=1, tiled=True)


def body(queries, key_rows, value_rows, parent):
    seq, head = lax.axis_size("seq"), lax.axis_size("head")
    if queries.shape[0] == BLOCK and head == 2 and seq % 4 == 0 and seq <= 16:
        return fused_body(queries, key_rows, value_rows, parent)
    return split_body(queries, key_rows, value_rows, parent)


def solution(mesh):
    return jax.shard_map(
        body,
        mesh=mesh,
        in_specs=(
            P(("seq", "head"), None),
            P(("seq", "head"), None),
            P(("seq", "head"), None),
            P(),
        ),
        out_specs=P(("seq", "head"), None),
        check_vma=False,
    )
```
